32 devices in a mesh: grid: 8 (over y, x, core), band: 4 (over z).
Axes of the slice: x: 2, y: 2, z: 4, core: 2. Of those that a mesh axis runs over, the one named last changes fastest.
Arguments:
- orbitals: float32 [256, 16, 8, 128], P('band', 'grid'), may hold values from -6 to 6
- potential: float32 [16, 8, 128], P('grid'), may hold values from -8 to 8
- rotation: float32 [256, 256], P(None, 'band'), may hold values from -0.375 to 0.375
Outputs:
- rotated: float32 [256, 16, 8, 128], P('band', 'grid')
The draws below stay inside these ranges and needn't reach their ends.
All inputs are finite; a program needn't handle non-finite values.
Results may differ from the reference program's by a relative error of at most 0.00007.
Values sent between devices are 32-bit elements; how exact they have to be, the bound alone decides.
A program may use at most 64 MiB of HBM per device.

```python
import jax
import jax.numpy as jnp
from jax import lax

ORB_DEV = 64
NY = 8
NZ = 128
NB = 256
NX = 16


def levels(stream_key, extent, shards, least, high):
    factor_of = 1.0
    for axis_at, parts in shards:
        heights = jax.random.uniform(jax.random.fold_in(jax.random.fold_in(stream_key, 6), axis_at), (parts,), jnp.float32, least / len(shards), high / len(shards))
        factor_of = factor_of * jnp.repeat(jnp.exp(heights), extent[axis_at] // parts).reshape((-1,) + (1,) * (len(extent) - 1 - axis_at))
    return factor_of


def normal_values(key, shape, width, bound, cuts=(), held_as=jnp.bfloat16):
    array = jax.random.normal(key, shape, jnp.float32) * width
    if len(cuts) > 0:
        array = levels(key, shape, cuts, -0.22, 0.18) * array
    return jnp.clip(array, min=-bound, max=bound).astype(held_as)


def setup_inputs(seed: int = 0) -> dict:
    key_of = jax.random.split(jax.random.key(seed), 4)
    return {
        "orbitals": normal_values(key_of[0], (NB, NX, NY, NZ), 1.0, 6.0, ((0, 4), (1, 8)), jnp.float32),
        "potential": jnp.clip(jax.random.uniform(key_of[1], (NX, NY, NZ), jnp.float32, -8.0, 8.0) * levels(key_of[1], (NX, NY, NZ), ((0, 8),), -0.4, 0.0), -8.0, 8.0),
        "rotation": normal_values(key_of[2], (NB, NB), NB ** -0.5, 0.375, ((1, 4),), jnp.float32),
    }


center_shift = 18.0
half_width = 16.0
spacing_square = 0.25


def second_along(states, which_axis):
    nearer = jnp.roll(states, 1, which_axis) + jnp.roll(states, -1, which_axis)
    farther = jnp.roll(states, 2, which_axis) + jnp.roll(states, -2, which_axis)
    return (16.0 * nearer - farther - 30.0 * states) / (12.0 * spacing_square)


def scaled_apply(states, potential):
    laplace = second_along(states, 1) + second_along(states, 2) + second_along(states, 3)
    hamilton = -0.5 * laplace + potential[None] * states
    return (hamilton - center_shift * states) / half_width


def filter_block(states, potential):
    scaled_once = scaled_apply(states, potential)
    return 2.0 * scaled_apply(scaled_once, potential) - states


def reference(orbitals, potential, rotation):
    blocks = orbitals.reshape(-1, ORB_DEV, NX, NY, NZ)

    def filter_one(block):
        return filter_block(block, potential)

    filtered = lax.map(filter_one, blocks)
    filtered = filtered.reshape(NB, NX * NY * NZ)
    rotated = jnp.dot(rotation.T, filtered, precision=lax.Precision.HIGHEST, preferred_element_type=jnp.float32)
    return rotated.reshape(NB, NX, NY, NZ)
```

```python
import functools

import jax
import jax.numpy as jnp
from jax import lax
from jax.experimental import pallas as pl
from jax.experimental.pallas import tpu as pltpu
from jax.sharding import PartitionSpec as P

center_shift = 18.0
half_width = 16.0
spacing_square = 0.25
MESH = pl.DeviceIdType.MESH


def padded_2(value, sides, width):
    for axis, dim in sides:
        devices, length = (lax.axis_size(axis), value.shape[dim])
        up = [(i, (i + 1) % devices) for i in range(devices)]
        down = [(j, i) for i, j in up]
        last = lax.slice_in_dim(value, length - width, length, axis=dim)
        leading = lax.slice_in_dim(value, 0, width, axis=dim)
        before = lax.ppermute(last, axis, up)
        after = lax.ppermute(leading, axis, down)
        value = jnp.concatenate([before, value, after], axis=dim)
    return value


def second_along(states, which_axis):
    nearer = jnp.roll(states, 1, which_axis) + jnp.roll(states, -1, which_axis)
    farther = jnp.roll(states, 2, which_axis) + jnp.roll(states, -2, which_axis)
    return (16.0 * nearer - farther - 30.0 * states) / (12.0 * spacing_square)


def scaled_apply(states, potential):
    padded = padded_2(states, (("grid", 1),), 2)
    thickness = states.shape[1]
    nearer = padded[:, 1 : thickness + 1] + padded[:, 3 : thickness + 3]
    farther = padded[:, 0:thickness] + padded[:, 4 : thickness + 4]
    along_x = (16.0 * nearer - farther - 30.0 * states) / (12.0 * spacing_square)
    laplace = along_x + second_along(states, 2) + second_along(states, 3)
    hamilton = -0.5 * laplace + potential[None] * states
    return (hamilton - center_shift * states) / half_width


def by_halos(orbitals, potential, rotation):
    scaled_once = scaled_apply(orbitals, potential)
    filtered = 2.0 * scaled_apply(scaled_once, potential) - orbitals
    columns = lax.all_gather(rotation, "band", axis=1, tiled=True)
    mixed_rows = jnp.einsum(
        "ob,oxyz->bxyz",
        columns,
        lax.all_to_all(filtered, "band", split_axis=3, concat_axis=0, tiled=True),
        precision=lax.Precision.HIGHEST,
    )
    return lax.all_to_all(mixed_rows, "band", split_axis=0, concat_axis=3, tiled=True)


near_factor = -0.5 * 16.0 / (12.0 * spacing_square) / half_width
far_factor = 0.5 / (12.0 * spacing_square) / half_width
own_factor = 0.5 * 90.0 / (12.0 * spacing_square) / half_width


def ring(value, by):
    by = by % value.shape[0]
    return jnp.concatenate([value[-by:], value[:-by]], axis=0)


def apply_once(v, diagonal):
    ny, nz = v.shape[1:]
    near = ring(v, 1) + ring(v, -1)
    far = ring(v, 2) + ring(v, -2)
    near = near + pltpu.roll(v, 1, 1) + pltpu.roll(v, ny - 1, 1)
    far = far + pltpu.roll(v, 2 % ny, 1) + pltpu.roll(v, (ny - 2) % ny, 1)
    near = near + pltpu.roll(v, 1, 2) + pltpu.roll(v, nz - 1, 2)
    far = far + pltpu.roll(v, 2, 2) + pltpu.roll(v, nz - 2, 2)
    return near_factor * near + far_factor * far + diagonal * v


def kernel(
    grid, band,
    orb_ref, pot_ref, rot_ref, out_ref,
    states, potentials, rotations, filtered, cells, turned, final,
    own_sem, orb_send, orb_recv, pot_send, pot_recv, rot_send, rot_recv,
    cell_send, cell_recv, fin_send, fin_recv,
):
    g, z = lax.axis_index("grid"), lax.axis_index("band")
    everyone = grid * band
    me = z * grid + g
    few = states.shape[0]
    planes, ny, nz = orb_ref.shape[1:]
    share = planes * ny // band
    mine = orb_ref.shape[0]

    barrier = pltpu.get_barrier_semaphore()

    def greet(d, _):
        to = lax.rem(me + d, everyone)
        pl.semaphore_signal(
            barrier, inc=1, device_id=(lax.rem(to, grid), to // grid), device_id_type=MESH
        )
        return _

    lax.fori_loop(1, everyone, greet, 0)

    own_orb = pltpu.make_async_copy(
        orb_ref.at[pl.ds(g * few, few)],
        states.at[:, pl.ds(g * planes, planes)],
        own_sem,
    )
    own_orb.start()
    potentials[pl.ds(g * planes, planes)] = pot_ref[...]
    rotations[z] = rot_ref[...]
    pl.semaphore_wait(barrier, everyone - 1)

    def orb_copy(d):
        to = lax.rem(g + d, grid)
        return pltpu.make_async_remote_copy(
            src_ref=orb_ref.at[pl.ds(to * few, few)],
            dst_ref=states.at[:, pl.ds(g * planes, planes)],
            send_sem=orb_send.at[d],
            recv_sem=orb_recv.at[d],
            device_id=(to, z),
            device_id_type=MESH,
        )

    def pot_copy(d):
        to = lax.rem(g + d, grid)
        return pltpu.make_async_remote_copy(
            src_ref=pot_ref,
            dst_ref=potentials.at[pl.ds(g * planes, planes)],
            send_sem=pot_send.at[d],
            recv_sem=pot_recv.at[d],
            device_id=(to, z),
            device_id_type=MESH,
        )

    def rot_copy(d):
        return pltpu.make_async_remote_copy(
            src_ref=rot_ref,
            dst_ref=rotations.at[z],
            send_sem=rot_send.at[d],
            recv_sem=rot_recv.at[d],
            device_id=(g, lax.rem(z + d, band)),
            device_id_type=MESH,
        )

    def cell_copy(d):
        to = lax.rem(me + d, everyone)
        row = (lax.rem(to, grid) * band + to // grid) * (share * few)
        return pltpu.make_async_remote_copy(
            src_ref=filtered.at[pl.ds(pl.multiple_of(row, 8), share * few)],
            dst_ref=cells.at[me],
            send_sem=cell_send.at[d],
            recv_sem=cell_recv.at[d],
            device_id=(lax.rem(to, grid), to // grid),
            device_id_type=MESH,
        )

    def fin_copy(d):
        to = lax.rem(z + d, band)
        return pltpu.make_async_remote_copy(
            src_ref=turned.at[to],
            dst_ref=final.at[z],
            send_sem=fin_send.at[d],
            recv_sem=fin_recv.at[d],
            device_id=(g, to),
            device_id_type=MESH,
        )

    def start_all(copy, count):
        def body(d, _):
            copy(d).start()
            return _

        lax.fori_loop(1, count, body, 0)

    def wait_all(copy, count):
        def body(d, _):
            copy(d).wait()
            return _

        lax.fori_loop(1, count, body, 0)

    start_all(pot_copy, grid)
    start_all(orb_copy, grid)
    start_all(rot_copy, band)
    own_orb.wait()
    wait_all(pot_copy, grid)
    wait_all(orb_copy, grid)

    diagonal = (potentials[...] - center_shift) / half_width + own_factor

    def filter_one(j, _):
        v = states[j]
        result = 2.0 * apply_once(apply_once(v, diagonal), diagonal) - v
        rows = result.shape[0] * ny
        filtered[pl.ds(j, rows, stride=few), :] = result.reshape(rows, nz)
        return _

    lax.fori_loop(0, few, filter_one, 0)

    start_all(cell_copy, everyone)
    row = (g * band + z) * (share * few)
    cells[me] = filtered[pl.ds(pl.multiple_of(row, 8), share * few), :]
    wait_all(rot_copy, band)
    wait_all(cell_copy, everyone)

    operand = jnp.concatenate(
        [
            cells[:, pl.ds(r * few, few), :].reshape(everyone * few, nz)
            for r in range(share)
        ],
        axis=1,
    )
    for d in list(range(1, band)) + [0]:
        to = lax.rem(z + d, band)
        part = lax.dot_general(
            rotations[to],
            operand,
            (((0,), (0,)), ((), ())),
            precision=lax.Precision.HIGHEST,
            preferred_element_type=jnp.float32,
        )
        for r in range(share):
            piece = part[:, r * nz : (r + 1) * nz]
            if d == 0:
                out_ref[pl.ds(z * share + r, mine, stride=planes * ny), :] = piece
            else:
                turned[to, pl.ds(r * mine, mine), :] = piece
        if d:
            fin_copy(d).start()
    for d in range(1, band):
        fin_copy(d).wait()
        of = lax.rem(z - d + band, band)
        for r in range(share):
            out_ref[pl.ds(of * share + r, mine, stride=planes * ny), :] = final[
                of, pl.ds(r * mine, mine), :
            ]


def by_exchange(grid, band, orbitals, potential, rotation):
    mine, planes, ny, nz = orbitals.shape
    few, share = mine // grid, planes * ny // band
    everyone = grid * band
    f32, dma = jnp.float32, pltpu.SemaphoreType.DMA
    vmem = pl.BlockSpec(memory_space=pltpu.VMEM)
    rotated = pl.pallas_call(
        functools.partial(kernel, grid, band),
        out_shape=jax.ShapeDtypeStruct((mine * planes * ny, nz), f32),
        in_specs=[pl.BlockSpec(memory_space=pl.ANY), vmem, vmem],
        out_specs=vmem,
        scratch_shapes=[
            pltpu.VMEM((few, grid * planes, ny, nz), f32),
            pltpu.VMEM((grid * planes, ny, nz), f32),
            pltpu.VMEM((band,) + rotation.shape, f32),
            pltpu.VMEM((grid * planes * ny * few, nz), f32),
            pltpu.VMEM((everyone, share * few, nz), f32),
            pltpu.VMEM((band, share * mine, nz), f32),
            pltpu.VMEM((band, share * mine, nz), f32),
            dma,
            dma((grid,)), dma((grid,)), dma((grid,)), dma((grid,)),
            dma((band,)), dma((band,)),
            dma((everyone,)), dma((everyone,)),
            dma((band,)), dma((band,)),
        ],
        compiler_params=pltpu.CompilerParams(
            collective_id=0, has_side_effects=True, vmem_limit_bytes=32 * 1024 * 1024
        ),
    )(orbitals, potential, rotation)
    return rotated.reshape(orbitals.shape)


def solution(mesh):
    grid, band = mesh.shape["grid"], mesh.shape["band"]

    def per_device(orbitals, potential, rotation):
        mine, planes, ny, _ = orbitals.shape
        if mine % (8 * grid) == 0 and planes * ny % band == 0:
            return by_exchange(grid, band, orbitals, potential, rotation)
        return by_halos(orbitals, potential, rotation)

    in_specs = (P("band", "grid", None, None), P("grid", None, None), P(None, "band"))
    out_specs = P("band", "grid", None, None)
    return jax.shard_map(
        per_device, mesh=mesh, in_specs=in_specs, out_specs=out_specs, check_vma=False
    )
```

```python
import functools

import jax
import jax.numpy as jnp
from jax import lax
from jax.experimental import pallas as pl
from jax.experimental.pallas import tpu as pltpu
from jax.sharding import PartitionSpec as P

center_shift = 18.0
half_width = 16.0
spacing_square = 0.25
MESH = pl.DeviceIdType.MESH


def padded_2(value, sides, width):
    for axis, dim in sides:
        devices, length = (lax.axis_size(axis), value.shape[dim])
        up = [(i, (i + 1) % devices) for i in range(devices)]
        down = [(j, i) for i, j in up]
        last = lax.slice_in_dim(value, length - width, length, axis=dim)
        leading = lax.slice_in_dim(value, 0, width, axis=dim)
        before = lax.ppermute(last, axis, up)
        after = lax.ppermute(leading, axis, down)
        value = jnp.concatenate([before, value, after], axis=dim)
    return value


def second_along(states, which_axis):
    nearer = jnp.roll(states, 1, which_axis) + jnp.roll(states, -1, which_axis)
    farther = jnp.roll(states, 2, which_axis) + jnp.roll(states, -2, which_axis)
    return (16.0 * nearer - farther - 30.0 * states) / (12.0 * spacing_square)


def scaled_apply(states, potential):
    padded = padded_2(states, (("grid", 1),), 2)
    thickness = states.shape[1]
    nearer = padded[:, 1 : thickness + 1] + padded[:, 3 : thickness + 3]
    farther = padded[:, 0:thickness] + padded[:, 4 : thickness + 4]
    along_x = (16.0 * nearer - farther - 30.0 * states) / (12.0 * spacing_square)
    laplace = along_x + second_along(states, 2) + second_along(states, 3)
    hamilton = -0.5 * laplace + potential[None] * states
    return (hamilton - center_shift * states) / half_width


def by_halos(orbitals, potential, rotation):
    scaled_once = scaled_apply(orbitals, potential)
    filtered = 2.0 * scaled_apply(scaled_once, potential) - orbitals
    columns = lax.all_gather(rotation, "band", axis=1, tiled=True)
    mixed_rows = jnp.einsum(
        "ob,oxyz->bxyz",
        columns,
        lax.all_to_all(filtered, "band", split_axis=3, concat_axis=0, tiled=True),
        precision=lax.Precision.HIGHEST,
    )
    return lax.all_to_all(mixed_rows, "band", split_axis=0, concat_axis=3, tiled=True)


near_factor = -0.5 * 16.0 / (12.0 * spacing_square) / half_width
far_factor = 0.5 / (12.0 * spacing_square) / half_width
own_factor = 0.5 * 90.0 / (12.0 * spacing_square) / half_width


def ring(value, by):
    by = by % value.shape[0]
    return jnp.concatenate([value[-by:], value[:-by]], axis=0)


def apply_once(v, diagonal):
    ny, nz = v.shape[1:]
    near = ring(v, 1) + ring(v, -1)
    far = ring(v, 2) + ring(v, -2)
    near = near + pltpu.roll(v, 1, 1) + pltpu.roll(v, ny - 1, 1)
    far = far + pltpu.roll(v, 2 % ny, 1) + pltpu.roll(v, (ny - 2) % ny, 1)
    near = near + pltpu.roll(v, 1, 2) + pltpu.roll(v, nz - 1, 2)
    far = far + pltpu.roll(v, 2, 2) + pltpu.roll(v, nz - 2, 2)
    return near_factor * near + far_factor * far + diagonal * v


def cell_rows(cells, share, part_of):
    chunks, everyone, _, nz = cells.shape
    if chunks == 1:
        return [
            cells[0, :, pl.ds(r * part_of, part_of), :].reshape(everyone * part_of, nz)
            for r in range(share)
        ]
    rows = []
    for pair in range(share // 2):
        first = cells[0, :, pl.ds(pair * 8, 8), :]
        second = cells[1, :, pl.ds(pair * 8, 8), :]
        low = lax.broadcasted_iota(jnp.int32, first.shape, 1) < 4
        even = jnp.where(low, first, pltpu.roll(second, 4, 1))
        odd = jnp.where(low, pltpu.roll(first, 4, 1), second)
        rows += [even.reshape(everyone * 8, nz), odd.reshape(everyone * 8, nz)]
    return rows


def kernel(
    grid, band,
    orb_ref, pot_ref, rot_ref, out_ref,
    states, potentials, rotations, filtered, cells, turned, final,
    own_sem, orb_send, orb_recv, pot_send, pot_recv, rot_send, rot_recv,
    spread_send, spread_recv, cell_send, cell_recv, fin_send, fin_recv,
):
    g, z = lax.axis_index("grid"), lax.axis_index("band")
    everyone = grid * band
    me = z * grid + g
    few = states.shape[0]
    chunks = filtered.shape[0]
    part_of = few // chunks
    planes, ny, nz = orb_ref.shape[1:]
    share = planes * ny // band
    mine = orb_ref.shape[0]

    barrier = pltpu.get_barrier_semaphore()

    def greet(d, _):
        to = lax.rem(me + d, everyone)
        pl.semaphore_signal(
            barrier, inc=1, device_id=(lax.rem(to, grid), to // grid), device_id_type=MESH
        )
        return _

    lax.fori_loop(1, everyone, greet, 0)

    own_orb = pltpu.make_async_copy(
        orb_ref.at[pl.ds(g * few, few)],
        states.at[:, pl.ds(g * planes, planes)],
        own_sem,
    )
    own_orb.start()
    potentials[pl.ds(g * planes, planes)] = pot_ref[...]
    rotations[z, pl.ds(g * few, few)] = rot_ref[pl.ds(pl.multiple_of(g * few, 8), few)]
    pl.semaphore_wait(barrier, everyone - 1)

    def orb_copy(c, d):
        to = lax.rem(g + d, grid)
        return pltpu.make_async_remote_copy(
            src_ref=orb_ref.at[pl.ds(to * few + c * part_of, part_of)],
            dst_ref=states.at[pl.ds(c * part_of, part_of), pl.ds(g * planes, planes)],
            send_sem=orb_send.at[c, d],
            recv_sem=orb_recv.at[c, d],
            device_id=(to, z),
            device_id_type=MESH,
        )

    def pot_copy(d):
        to = lax.rem(g + d, grid)
        return pltpu.make_async_remote_copy(
            src_ref=pot_ref,
            dst_ref=potentials.at[pl.ds(g * planes, planes)],
            send_sem=pot_send.at[d],
            recv_sem=pot_recv.at[d],
            device_id=(to, z),
            device_id_type=MESH,
        )

    def rot_copy(d):
        return pltpu.make_async_remote_copy(
            src_ref=rot_ref.at[pl.ds(g * few, few)],
            dst_ref=rotations.at[z, pl.ds(g * few, few)],
            send_sem=rot_send.at[d],
            recv_sem=rot_recv.at[d],
            device_id=(g, lax.rem(z + d, band)),
            device_id_type=MESH,
        )

    def spread_copy(d):
        rows = rotations.at[:, pl.ds(g * few, few)]
        return pltpu.make_async_remote_copy(
            src_ref=rows,
            dst_ref=rows,
            send_sem=spread_send.at[d],
            recv_sem=spread_recv.at[d],
            device_id=(lax.rem(g + d, grid), z),
            device_id_type=MESH,
        )

    def cell_copy(c, d):
        to = lax.rem(me + d, everyone)
        row = (lax.rem(to, grid) * band + to // grid) * (share * part_of)
        return pltpu.make_async_remote_copy(
            src_ref=filtered.at[c, pl.ds(pl.multiple_of(row, 8), share * part_of)],
            dst_ref=cells.at[c, me],
            send_sem=cell_send.at[c, d],
            recv_sem=cell_recv.at[c, d],
            device_id=(lax.rem(to, grid), to // grid),
            device_id_type=MESH,
        )

    def fin_copy(d):
        to = lax.rem(z + d, band)
        return pltpu.make_async_remote_copy(
            src_ref=turned.at[to],
            dst_ref=final.at[z],
            send_sem=fin_send.at[d],
            recv_sem=fin_recv.at[d],
            device_id=(g, to),
            device_id_type=MESH,
        )

    def start_all(copy, count):
        def body(d, _):
            copy(d).start()
            return _

        lax.fori_loop(1, count, body, 0)

    def wait_all(copy, count):
        def body(d, _):
            copy(d).wait()
            return _

        lax.fori_loop(1, count, body, 0)

    start_all(rot_copy, band)
    start_all(pot_copy, grid)
    for c in range(chunks):
        start_all(functools.partial(orb_copy, c), grid)
    own_orb.wait()
    wait_all(pot_copy, grid)
    diagonal = (potentials[...] - center_shift) / half_width + own_factor
    own_row = pl.multiple_of((g * band + z) * (share * part_of), 8)
    for c in range(chunks):
        wait_all(functools.partial(orb_copy, c), grid)

        def filter_one(j, _):
            v = states[c * part_of + j]
            result = 2.0 * apply_once(apply_once(v, diagonal), diagonal) - v
            rows = result.shape[0] * ny
            filtered[c, pl.ds(j, rows, stride=part_of), :] = result.reshape(rows, nz)
            return _

        lax.fori_loop(0, part_of, filter_one, 0)
        start_all(functools.partial(cell_copy, c), everyone)
        cells[c, me] = filtered[c, pl.ds(own_row, share * part_of), :]

    wait_all(rot_copy, band)
    start_all(spread_copy, grid)
    wait_all(spread_copy, grid)
    for c in range(chunks):
        wait_all(functools.partial(cell_copy, c), everyone)

    operand = jnp.concatenate(cell_rows(cells, share, part_of), axis=1)
    for d in list(range(1, band)) + [0]:
        to = lax.rem(z + d, band)
        part = lax.dot_general(
            rotations[to],
            operand,
            (((1,), (0,)), ((), ())),
            precision=lax.Precision.HIGHEST,
            preferred_element_type=jnp.float32,
        )
        for r in range(share):
            piece = part[:, r * nz : (r + 1) * nz]
            if d == 0:
                out_ref[pl.ds(z * share + r, mine, stride=planes * ny), :] = piece
            else:
                turned[to, pl.ds(r * mine, mine), :] = piece
        if d:
            fin_copy(d).start()
    for d in range(1, band):
        fin_copy(d).wait()
        of = lax.rem(z - d + band, band)
        for r in range(share):
            out_ref[pl.ds(of * share + r, mine, stride=planes * ny), :] = final[
                of, pl.ds(r * mine, mine), :
            ]


def by_exchange(grid, band, orbitals, potential, rotation):
    mine, planes, ny, nz = orbitals.shape
    few, share = mine // grid, planes * ny // band
    everyone = grid * band
    f32, dma = jnp.float32, pltpu.SemaphoreType.DMA
    chunks = 2 if few == 8 and share % 2 == 0 else 1
    vmem = pl.BlockSpec(memory_space=pltpu.VMEM)
    rotated = pl.pallas_call(
        functools.partial(kernel, grid, band),
        out_shape=jax.ShapeDtypeStruct((mine * planes * ny, nz), f32),
        in_specs=[pl.BlockSpec(memory_space=pl.ANY), vmem, vmem],
        out_specs=vmem,
        scratch_shapes=[
            pltpu.VMEM((few, grid * planes, ny, nz), f32),
            pltpu.VMEM((grid * planes, ny, nz), f32),
            pltpu.VMEM((band,) + rotation.shape[::-1], f32),
            pltpu.VMEM((chunks, grid * planes * ny * few // chunks, nz), f32),
            pltpu.VMEM((chunks, everyone, share * few // chunks, nz), f32),
            pltpu.VMEM((band, share * mine, nz), f32),
            pltpu.VMEM((band, share * mine, nz), f32),
            dma,
            dma((chunks, grid)), dma((chunks, grid)), dma((grid,)), dma((grid,)),
            dma((band,)), dma((band,)), dma((grid,)), dma((grid,)),
            dma((chunks, everyone)), dma((chunks, everyone)),
            dma((band,)), dma((band,)),
        ],
        compiler_params=pltpu.CompilerParams(
            collective_id=0, has_side_effects=True, vmem_limit_bytes=32 * 1024 * 1024
        ),
    )(orbitals, potential, rotation.T)
    return rotated.reshape(orbitals.shape)


def solution(mesh):
    grid, band = mesh.shape["grid"], mesh.shape["band"]

    def per_device(orbitals, potential, rotation):
        mine, planes, ny, _ = orbitals.shape
        if mine % (8 * grid) == 0 and planes * ny % band == 0:
            return by_exchange(grid, band, orbitals, potential, rotation)
        return by_halos(orbitals, potential, rotation)

    in_specs = (P("band", "grid", None, None), P("grid", None, None), P(None, "band"))
    out_specs = P("band", "grid", None, None)
    return jax.shard_map(
        per_device, mesh=mesh, in_specs=in_specs, out_specs=out_specs, check_vma=False
    )
```

```python
import functools

import jax
import jax.numpy as jnp
from jax import lax
from jax.experimental import pallas as pl
from jax.experimental.pallas import tpu as pltpu
from jax.sharding import PartitionSpec as P

center_shift = 18.0
half_width = 16.0
spacing_square = 0.25
MESH = pl.DeviceIdType.MESH


def padded_2(value, sides, width):
    for axis, dim in sides:
        devices, length = (lax.axis_size(axis), value.shape[dim])
        up = [(i, (i + 1) % devices) for i in range(devices)]
        down = [(j, i) for i, j in up]
        last = lax.slice_in_dim(value, length - width, length, axis=dim)
        leading = lax.slice_in_dim(value, 0, width, axis=dim)
        before = lax.ppermute(last, axis, up)
        after = lax.ppermute(leading, axis, down)
        value = jnp.concatenate([before, value, after], axis=dim)
    return value


def second_along(states, which_axis):
    nearer = jnp.roll(states, 1, which_axis) + jnp.roll(states, -1, which_axis)
    farther = jnp.roll(states, 2, which_axis) + jnp.roll(states, -2, which_axis)
    return (16.0 * nearer - farther - 30.0 * states) / (12.0 * spacing_square)


def scaled_apply(states, potential):
    padded = padded_2(states, (("grid", 1),), 2)
    thickness = states.shape[1]
    nearer = padded[:, 1 : thickness + 1] + padded[:, 3 : thickness + 3]
    farther = padded[:, 0:thickness] + padded[:, 4 : thickness + 4]
    along_x = (16.0 * nearer - farther - 30.0 * states) / (12.0 * spacing_square)
    laplace = along_x + second_along(states, 2) + second_along(states, 3)
    hamilton = -0.5 * laplace + potential[None] * states
    return (hamilton - center_shift * states) / half_width


def by_halos(orbitals, potential, rotation):
    scaled_once = scaled_apply(orbitals, potential)
    filtered = 2.0 * scaled_apply(scaled_once, potential) - orbitals
    columns = lax.all_gather(rotation, "band", axis=1, tiled=True)
    mixed_rows = jnp.einsum(
        "ob,oxyz->bxyz",
        columns,
        lax.all_to_all(filtered, "band", split_axis=3, concat_axis=0, tiled=True),
        precision=lax.Precision.HIGHEST,
    )
    return lax.all_to_all(mixed_rows, "band", split_axis=0, concat_axis=3, tiled=True)


near_factor = -0.5 * 16.0 / (12.0 * spacing_square) / half_width
far_factor = 0.5 / (12.0 * spacing_square) / half_width
own_factor = 0.5 * 90.0 / (12.0 * spacing_square) / half_width


def ring(value, by):
    by = by % value.shape[0]
    return jnp.concatenate([value[-by:], value[:-by]], axis=0)


def apply_once(v, diagonal):
    ny, nz = v.shape[1:]
    near = ring(v, 1) + ring(v, -1)
    far = ring(v, 2) + ring(v, -2)
    near = near + pltpu.roll(v, 1, 1) + pltpu.roll(v, ny - 1, 1)
    far = far + pltpu.roll(v, 2 % ny, 1) + pltpu.roll(v, (ny - 2) % ny, 1)
    near = near + pltpu.roll(v, 1, 2) + pltpu.roll(v, nz - 1, 2)
    far = far + pltpu.roll(v, 2, 2) + pltpu.roll(v, nz - 2, 2)
    return near_factor * near + far_factor * far + diagonal * v


def cell_rows(cells, share, part_of):
    chunks, everyone, _, nz = cells.shape
    if chunks == 1:
        return [
            cells[0, :, pl.ds(r * part_of, part_of), :].reshape(everyone * part_of, nz)
            for r in range(share)
        ]
    rows = []
    for pair in range(share // 2):
        first = cells[0, :, pl.ds(pair * 8, 8), :]
        second = cells[1, :, pl.ds(pair * 8, 8), :]
        low = lax.broadcasted_iota(jnp.int32, first.shape, 1) < 4
        even = jnp.where(low, first, pltpu.roll(second, 4, 1))
        odd = jnp.where(low, pltpu.roll(first, 4, 1), second)
        rows += [even.reshape(everyone * 8, nz), odd.reshape(everyone * 8, nz)]
    return rows


def halves(value):
    high = value.astype(jnp.bfloat16)
    return high, (value - high.astype(jnp.float32)).astype(jnp.bfloat16)


def dot(a, b):
    return lax.dot_general(
        a, b, (((1,), (0,)), ((), ())), preferred_element_type=jnp.float32
    )


def kernel(
    grid, band,
    orb_ref, pot_ref, rot_ref, out_ref,
    states, potentials, rotations, filtered, cells, turned, final,
    own_sem, orb_send, orb_recv, pot_send, pot_recv, rot_send, rot_recv,
    spread_send, spread_recv, cell_send, cell_recv, fin_send, fin_recv,
):
    g, z = lax.axis_index("grid"), lax.axis_index("band")
    everyone = grid * band
    me = z * grid + g
    few = states.shape[0]
    chunks = filtered.shape[0]
    part_of = few // chunks
    planes, ny, nz = orb_ref.shape[1:]
    share = planes * ny // band
    mine = orb_ref.shape[0]

    barrier = pltpu.get_barrier_semaphore()

    def greet(d, _):
        to = lax.rem(me + d, everyone)
        pl.semaphore_signal(
            barrier, inc=1, device_id=(lax.rem(to, grid), to // grid), device_id_type=MESH
        )
        return _

    lax.fori_loop(1, everyone, greet, 0)

    own_orb = pltpu.make_async_copy(
        orb_ref.at[pl.ds(g * few, few)],
        states.at[:, pl.ds(g * planes, planes)],
        own_sem,
    )
    own_orb.start()
    potentials[pl.ds(g * planes, planes)] = pot_ref[...]
    rotations[z, pl.ds(g * few, few)] = rot_ref[pl.ds(pl.multiple_of(g * few, 8), few)]
    pl.semaphore_wait(barrier, everyone - 1)

    def orb_copy(c, d):
        to = lax.rem(g + d, grid)
        return pltpu.make_async_remote_copy(
            src_ref=orb_ref.at[pl.ds(to * few + c * part_of, part_of)],
            dst_ref=states.at[pl.ds(c * part_of, part_of), pl.ds(g * planes, planes)],
            send_sem=orb_send.at[c, d],
            recv_sem=orb_recv.at[c, d],
            device_id=(to, z),
            device_id_type=MESH,
        )

    def pot_copy(d):
        to = lax.rem(g + d, grid)
        return pltpu.make_async_remote_copy(
            src_ref=pot_ref,
            dst_ref=potentials.at[pl.ds(g * planes, planes)],
            send_sem=pot_send.at[d],
            recv_sem=pot_recv.at[d],
            device_id=(to, z),
            device_id_type=MESH,
        )

    def rot_copy(d):
        return pltpu.make_async_remote_copy(
            src_ref=rot_ref.at[pl.ds(g * few, few)],
            dst_ref=rotations.at[z, pl.ds(g * few, few)],
            send_sem=rot_send.at[d],
            recv_sem=rot_recv.at[d],
            device_id=(g, lax.rem(z + d, band)),
            device_id_type=MESH,
        )

    def spread_copy(d):
        rows = rotations.at[:, pl.ds(g * few, few)]
        return pltpu.make_async_remote_copy(
            src_ref=rows,
            dst_ref=rows,
            send_sem=spread_send.at[d],
            recv_sem=spread_recv.at[d],
            device_id=(lax.rem(g + d, grid), z),
            device_id_type=MESH,
        )

    def cell_copy(c, d):
        to = lax.rem(me + d, everyone)
        row = (lax.rem(to, grid) * band + to // grid) * (share * part_of)
        return pltpu.make_async_remote_copy(
            src_ref=filtered.at[c, pl.ds(pl.multiple_of(row, 8), share * part_of)],
            dst_ref=cells.at[c, me],
            send_sem=cell_send.at[c, d],
            recv_sem=cell_recv.at[c, d],
            device_id=(lax.rem(to, grid), to // grid),
            device_id_type=MESH,
        )

    def fin_copy(d):
        to = lax.rem(z + d, band)
        return pltpu.make_async_remote_copy(
            src_ref=turned.at[to],
            dst_ref=final.at[z],
            send_sem=fin_send.at[d],
            recv_sem=fin_recv.at[d],
            device_id=(g, to),
            device_id_type=MESH,
        )

    def start_all(copy, count):
        for d in range(1, count):
            copy(d).start()

    def wait_all(copy, count):
        for d in range(1, count):
            copy(d).wait()

    start_all(rot_copy, band)
    start_all(pot_copy, grid)
    for c in range(chunks):
        start_all(functools.partial(orb_copy, c), grid)
    own_orb.wait()
    wait_all(pot_copy, grid)
    diagonal = (potentials[...] - center_shift) / half_width + own_factor
    own_row = pl.multiple_of((g * band + z) * (share * part_of), 8)
    for c in range(chunks):
        wait_all(functools.partial(orb_copy, c), grid)

        def filter_one(j, _):
            v = states[c * part_of + j]
            result = 2.0 * apply_once(apply_once(v, diagonal), diagonal) - v
            rows = result.shape[0] * ny
            filtered[c, pl.ds(j, rows, stride=part_of), :] = result.reshape(rows, nz)
            return _

        lax.fori_loop(0, part_of, filter_one, 0)
        start_all(functools.partial(cell_copy, c), everyone)
        cells[c, me] = filtered[c, pl.ds(own_row, share * part_of), :]

    wait_all(rot_copy, band)
    start_all(spread_copy, grid)
    wait_all(spread_copy, grid)
    for c in range(chunks):
        wait_all(functools.partial(cell_copy, c), everyone)

    high, low = halves(jnp.concatenate(cell_rows(cells, share, part_of), axis=1))
    for d in list(range(1, band)) + [0]:
        to = lax.rem(z + d, band)
        turn_high, turn_low = halves(rotations[to])
        part = (
            dot(turn_low, high) + dot(turn_high, low) + dot(turn_high, high)
        )
        for r in range(share):
            piece = part[:, r * nz : (r + 1) * nz]
            if d == 0:
                out_ref[pl.ds(z * share + r, mine, stride=planes * ny), :] = piece
            else:
                turned[to, pl.ds(r * mine, mine), :] = piece
        if d:
            fin_copy(d).start()
    for d in range(1, band):
        fin_copy(d).wait()
        of = lax.rem(z - d + band, band)
        for r in range(share):
            out_ref[pl.ds(of * share + r, mine, stride=planes * ny), :] = final[
                of, pl.ds(r * mine, mine), :
            ]


def by_exchange(grid, band, orbitals, potential, rotation):
    mine, planes, ny, nz = orbitals.shape
    few, share = mine // grid, planes * ny // band
    everyone = grid * band
    f32, dma = jnp.float32, pltpu.SemaphoreType.DMA
    chunks = 2 if few == 8 and share % 2 == 0 else 1
    vmem = pl.BlockSpec(memory_space=pltpu.VMEM)
    rotated = pl.pallas_call(
        functools.partial(kernel, grid, band),
        out_shape=jax.ShapeDtypeStruct((mine * planes * ny, nz), f32),
        in_specs=[pl.BlockSpec(memory_space=pl.ANY), vmem, vmem],
        out_specs=vmem,
        scratch_shapes=[
            pltpu.VMEM((few, grid * planes, ny, nz), f32),
            pltpu.VMEM((grid * planes, ny, nz), f32),
            pltpu.VMEM((band,) + rotation.shape[::-1], f32),
            pltpu.VMEM((chunks, grid * planes * ny * few // chunks, nz), f32),
            pltpu.VMEM((chunks, everyone, share * few // chunks, nz), f32),
            pltpu.VMEM((band, share * mine, nz), f32),
            pltpu.VMEM((band, share * mine, nz), f32),
            dma,
            dma((chunks, grid)), dma((chunks, grid)), dma((grid,)), dma((grid,)),
            dma((band,)), dma((band,)), dma((grid,)), dma((grid,)),
            dma((chunks, everyone)), dma((chunks, everyone)),
            dma((band,)), dma((band,)),
        ],
        compiler_params=pltpu.CompilerParams(
            collective_id=0, has_side_effects=True, vmem_limit_bytes=32 * 1024 * 1024
        ),
    )(orbitals, potential, rotation.T)
    return rotated.reshape(orbitals.shape)


def solution(mesh):
    grid, band = mesh.shape["grid"], mesh.shape["band"]

    def per_device(orbitals, potential, rotation):
        mine, planes, ny, _ = orbitals.shape
        if mine % (8 * grid) == 0 and planes * ny % band == 0:
            return by_exchange(grid, band, orbitals, potential, rotation)
        return by_halos(orbitals, potential, rotation)

    in_specs = (P("band", "grid", None, None), P("grid", None, None), P(None, "band"))
    out_specs = P("band", "grid", None, None)
    return jax.shard_map(
        per_device, mesh=mesh, in_specs=in_specs, out_specs=out_specs, check_vma=False
    )
```

```python
import functools

import jax
import jax.numpy as jnp
from jax import lax
from jax.experimental import pallas as pl
from jax.experimental.pallas import tpu as pltpu
from jax.sharding import PartitionSpec as P

center_shift = 18.0
half_width = 16.0
spacing_square = 0.25
MESH = pl.DeviceIdType.MESH


def padded_2(value, sides, width):
    for axis, dim in sides:
        devices, length = (lax.axis_size(axis), value.shape[dim])
        up = [(i, (i + 1) % devices) for i in range(devices)]
        down = [(j, i) for i, j in up]
        last = lax.slice_in_dim(value, length - width, length, axis=dim)
        leading = lax.slice_in_dim(value, 0, width, axis=dim)
        before = lax.ppermute(last, axis, up)
        after = lax.ppermute(leading, axis, down)
        value = jnp.concatenate([before, value, after], axis=dim)
    return value


def second_along(states, which_axis):
    nearer = jnp.roll(states, 1, which_axis) + jnp.roll(states, -1, which_axis)
    farther = jnp.roll(states, 2, which_axis) + jnp.roll(states, -2, which_axis)
    return (16.0 * nearer - farther - 30.0 * states) / (12.0 * spacing_square)


def scaled_apply(states, potential):
    padded = padded_2(states, (("grid", 1),), 2)
    thickness = states.shape[1]
    nearer = padded[:, 1 : thickness + 1] + padded[:, 3 : thickness + 3]
    farther = padded[:, 0:thickness] + padded[:, 4 : thickness + 4]
    along_x = (16.0 * nearer - farther - 30.0 * states) / (12.0 * spacing_square)
    laplace = along_x + second_along(states, 2) + second_along(states, 3)
    hamilton = -0.5 * laplace + potential[None] * states
    return (hamilton - center_shift * states) / half_width


def by_halos(orbitals, potential, rotation):
    scaled_once = scaled_apply(orbitals, potential)
    filtered = 2.0 * scaled_apply(scaled_once, potential) - orbitals
    columns = lax.all_gather(rotation, "band", axis=1, tiled=True)
    mixed_rows = jnp.einsum(
        "ob,oxyz->bxyz",
        columns,
        lax.all_to_all(filtered, "band", split_axis=3, concat_axis=0, tiled=True),
        precision=lax.Precision.HIGHEST,
    )
    return lax.all_to_all(mixed_rows, "band", split_axis=0, concat_axis=3, tiled=True)


near_factor = -0.5 * 16.0 / (12.0 * spacing_square) / half_width
far_factor = 0.5 / (12.0 * spacing_square) / half_width
own_factor = 0.5 * 90.0 / (12.0 * spacing_square) / half_width


def ring(value, by):
    by = by % value.shape[0]
    return jnp.concatenate([value[-by:], value[:-by]], axis=0)


def apply_once(v, diagonal):
    ny, nz = v.shape[1:]
    near = ring(v, 1) + ring(v, -1)
    far = ring(v, 2) + ring(v, -2)
    near = near + pltpu.roll(v, 1, 1) + pltpu.roll(v, ny - 1, 1)
    far = far + pltpu.roll(v, 2 % ny, 1) + pltpu.roll(v, (ny - 2) % ny, 1)
    near = near + pltpu.roll(v, 1, 2) + pltpu.roll(v, nz - 1, 2)
    far = far + pltpu.roll(v, 2, 2) + pltpu.roll(v, nz - 2, 2)
    return near_factor * near + far_factor * far + diagonal * v


def cell_rows(cells, share, part_of):
    chunks, everyone, _, nz = cells.shape
    if chunks == 1:
        return [
            cells[0, :, pl.ds(r * part_of, part_of), :].reshape(everyone * part_of, nz)
            for r in range(share)
        ]
    rows = []
    for pair in range(share // 2):
        first = cells[0, :, pl.ds(pair * 8, 8), :]
        second = cells[1, :, pl.ds(pair * 8, 8), :]
        low = lax.broadcasted_iota(jnp.int32, first.shape, 1) < 4
        even = jnp.where(low, first, pltpu.roll(second, 4, 1))
        odd = jnp.where(low, pltpu.roll(first, 4, 1), second)
        rows += [even.reshape(everyone * 8, nz), odd.reshape(everyone * 8, nz)]
    return rows


def halves(value):
    high = value.astype(jnp.bfloat16)
    return high, (value - high.astype(jnp.float32)).astype(jnp.bfloat16)


def dot(a, b):
    return lax.dot_general(
        a, b, (((1,), (0,)), ((), ())), preferred_element_type=jnp.float32
    )


def kernel(
    grid, band,
    orb_ref, pot_ref, rot_ref, out_ref,
    states, potentials, rotations, filtered, cells, turned, final,
    own_sem, orb_send, orb_recv, pot_send, pot_recv, rot_send, rot_recv,
    spread_send, spread_recv, cell_send, cell_recv, fin_send, fin_recv,
):
    g, z = lax.axis_index("grid"), lax.axis_index("band")
    everyone = grid * band
    me = z * grid + g
    few = states.shape[0]
    chunks = filtered.shape[0]
    part_of = few // chunks
    planes, ny, nz = orb_ref.shape[1:]
    share = planes * ny // band
    mine = orb_ref.shape[0]

    barrier = pltpu.get_barrier_semaphore()

    def greet(d, _):
        to = lax.rem(me + d, everyone)
        pl.semaphore_signal(
            barrier, inc=1, device_id=(lax.rem(to, grid), to // grid), device_id_type=MESH
        )
        return _

    lax.fori_loop(1, everyone, greet, 0)

    own_orb = pltpu.make_async_copy(
        orb_ref.at[pl.ds(g * few, few)],
        states.at[:, pl.ds(g * planes, planes)],
        own_sem,
    )
    own_orb.start()
    potentials[pl.ds(g * planes, planes)] = pot_ref[...]
    rotations[z, pl.ds(g * few, few)] = rot_ref[pl.ds(pl.multiple_of(g * few, 8), few)]
    pl.semaphore_wait(barrier, everyone - 1)

    def orb_copy(c, d):
        to = lax.rem(g + d, grid)
        return pltpu.make_async_remote_copy(
            src_ref=orb_ref.at[pl.ds(to * few + c * part_of, part_of)],
            dst_ref=states.at[pl.ds(c * part_of, part_of), pl.ds(g * planes, planes)],
            send_sem=orb_send.at[c, d],
            recv_sem=orb_recv.at[c, d],
            device_id=(to, z),
            device_id_type=MESH,
        )

    def pot_copy(d):
        to = lax.rem(g + d, grid)
        return pltpu.make_async_remote_copy(
            src_ref=pot_ref,
            dst_ref=potentials.at[pl.ds(g * planes, planes)],
            send_sem=pot_send.at[d],
            recv_sem=pot_recv.at[d],
            device_id=(to, z),
            device_id_type=MESH,
        )

    def rot_copy(d):
        return pltpu.make_async_remote_copy(
            src_ref=rot_ref.at[pl.ds(g * few, few)],
            dst_ref=rotations.at[z, pl.ds(g * few, few)],
            send_sem=rot_send.at[d],
            recv_sem=rot_recv.at[d],
            device_id=(g, lax.rem(z + d, band)),
            device_id_type=MESH,
        )

    def spread_copy(d):
        rows = rotations.at[:, pl.ds(g * few, few)]
        return pltpu.make_async_remote_copy(
            src_ref=rows,
            dst_ref=rows,
            send_sem=spread_send.at[d],
            recv_sem=spread_recv.at[d],
            device_id=(lax.rem(g + d, grid), z),
            device_id_type=MESH,
        )

    def cell_copy(c, d):
        to = lax.rem(me + d, everyone)
        row = (lax.rem(to, grid) * band + to // grid) * (share * part_of)
        return pltpu.make_async_remote_copy(
            src_ref=filtered.at[c, pl.ds(pl.multiple_of(row, 8), share * part_of)],
            dst_ref=cells.at[c, me],
            send_sem=cell_send.at[c, d],
            recv_sem=cell_recv.at[c, d],
            device_id=(lax.rem(to, grid), to // grid),
            device_id_type=MESH,
        )

    def fin_copy(d):
        to = lax.rem(z + d, band)
        return pltpu.make_async_remote_copy(
            src_ref=turned.at[to],
            dst_ref=final.at[z],
            send_sem=fin_send.at[d],
            recv_sem=fin_recv.at[d],
            device_id=(g, to),
            device_id_type=MESH,
        )

    def start_all(copy, count):
        for d in range(1, count):
            copy(d).start()

    def wait_all(copy, count):
        for d in range(1, count):
            copy(d).wait()

    start_all(pot_copy, grid)
    start_all(functools.partial(orb_copy, 0), grid)
    start_all(rot_copy, band)
    own_orb.wait()
    wait_all(pot_copy, grid)
    for c in range(1, chunks):
        start_all(functools.partial(orb_copy, c), grid)
    diagonal = (potentials[...] - center_shift) / half_width + own_factor
    own_row = pl.multiple_of((g * band + z) * (share * part_of), 8)
    for c in range(chunks):
        wait_all(functools.partial(orb_copy, c), grid)

        def filter_one(j, _):
            v = states[c * part_of + j]
            result = 2.0 * apply_once(apply_once(v, diagonal), diagonal) - v
            rows = result.shape[0] * ny
            filtered[c, pl.ds(j, rows, stride=part_of), :] = result.reshape(rows, nz)
            return _

        lax.fori_loop(0, part_of, filter_one, 0)
        start_all(functools.partial(cell_copy, c), everyone)
        cells[c, me] = filtered[c, pl.ds(own_row, share * part_of), :]

    wait_all(rot_copy, band)
    start_all(spread_copy, grid)
    wait_all(spread_copy, grid)
    for c in range(chunks):
        wait_all(functools.partial(cell_copy, c), everyone)

    high, low = halves(jnp.concatenate(cell_rows(cells, share, part_of), axis=1))
    for d in list(range(1, band)) + [0]:
        to = lax.rem(z + d, band)
        turn_high, turn_low = halves(rotations[to])
        part = (
            dot(turn_low, high) + dot(turn_high, low) + dot(turn_high, high)
        )
        for r in range(share):
            piece = part[:, r * nz : (r + 1) * nz]
            if d == 0:
                out_ref[pl.ds(z * share + r, mine, stride=planes * ny), :] = piece
            else:
                turned[to, pl.ds(r * mine, mine), :] = piece
        if d:
            fin_copy(d).start()
    for d in range(1, band):
        fin_copy(d).wait()
        of = lax.rem(z - d + band, band)
        for r in range(share):
            out_ref[pl.ds(of * share + r, mine, stride=planes * ny), :] = final[
                of, pl.ds(r * mine, mine), :
            ]


def by_exchange(grid, band, orbitals, potential, rotation):
    mine, planes, ny, nz = orbitals.shape
    few, share = mine // grid, planes * ny // band
    everyone = grid * band
    f32, dma = jnp.float32, pltpu.SemaphoreType.DMA
    chunks = 2 if few == 8 and share % 2 == 0 else 1
    vmem = pl.BlockSpec(memory_space=pltpu.VMEM)
    rotated = pl.pallas_call(
        functools.partial(kernel, grid, band),
        out_shape=jax.ShapeDtypeStruct((mine * planes * ny, nz), f32),
        in_specs=[pl.BlockSpec(memory_space=pl.ANY), vmem, vmem],
        out_specs=vmem,
        scratch_shapes=[
            pltpu.VMEM((few, grid * planes, ny, nz), f32),
            pltpu.VMEM((grid * planes, ny, nz), f32),
            pltpu.VMEM((band,) + rotation.shape[::-1], f32),
            pltpu.VMEM((chunks, grid * planes * ny * few // chunks, nz), f32),
            pltpu.VMEM((chunks, everyone, share * few // chunks, nz), f32),
            pltpu.VMEM((band, share * mine, nz), f32),
            pltpu.VMEM((band, share * mine, nz), f32),
            dma,
            dma((chunks, grid)), dma((chunks, grid)), dma((grid,)), dma((grid,)),
            dma((band,)), dma((band,)), dma((grid,)), dma((grid,)),
            dma((chunks, everyone)), dma((chunks, everyone)),
            dma((band,)), dma((band,)),
        ],
        compiler_params=pltpu.CompilerParams(
            collective_id=0, has_side_effects=True, vmem_limit_bytes=32 * 1024 * 1024
        ),
    )(orbitals, potential, rotation.T)
    return rotated.reshape(orbitals.shape)


def solution(mesh):
    grid, band = mesh.shape["grid"], mesh.shape["band"]

    def per_device(orbitals, potential, rotation):
        mine, planes, ny, _ = orbitals.shape
        if mine % (8 * grid) == 0 and planes * ny % band == 0:
            return by_exchange(grid, band, orbitals, potential, rotation)
        return by_halos(orbitals, potential, rotation)

    in_specs = (P("band", "grid", None, None), P("grid", None, None), P(None, "band"))
    out_specs = P("band", "grid", None, None)
    return jax.shard_map(
        per_device, mesh=mesh, in_specs=in_specs, out_specs=out_specs, check_vma=False
    )
```
